32 devices in a mesh: member: 2 (over x), lat: 16 (over z, y, core).
Axes of the slice: x: 2, y: 2, z: 4, core: 2. Of those that a mesh axis runs over, the one named last changes fastest.
Arguments:
- field: bfloat16 [512, 64, 256], P(('member', 'lat')), parts along dimension 0, may hold values from -6 to 6
- row_start: int32 [256], P('lat'), may hold values from 0 to 250, as said below
- row_count: int32 [256], P('lat'), may hold values from 6 to 13
- tap_count: int32 [256], P('lat'), may hold values from 3 to 7, as said below
- basis: bfloat16 [256, 13, 7, 9], P('lat'), may hold values from -2 to 2
- mixing: bfloat16 [2304, 256], replicated, may hold values from -0.125 to 0.125
- cotangent: bfloat16 [512, 64, 256], P(('member', 'lat')), parts along dimension 0, may hold values from -6 to 6
Outputs:
- hidden: bfloat16 [512, 64, 256], P(('member', 'lat')), parts along dimension 0
- field_grad: bfloat16 [512, 64, 256], P(('member', 'lat')), parts along dimension 0
- mixing_grad: float32 [4608, 256], P(('member', 'lat')), parts along dimension 0
The draws below stay inside these ranges and needn't reach their ends.
There are 2 independent parts, one for each index of `member`. The reference program is written for one: setup_inputs(seed, part) draws one part's arguments, and reference() takes and returns one part's arrays. A program takes and returns all parts, laid end to end along the dimension named above; an argument that names none is the same for every part. Nothing has to cross between parts.
Inputs may be any that keep to these rules, and one draw needn't show every extreme that they name: Output row o reads input rows row_start[o] to row_start[o] + row_count[o] - 1; they contain o and lie within 6 rows of it. `tap_count`: Odd; wider toward the poles.
All inputs are finite; a program needn't handle non-finite values.
Results may differ from the reference program's by a relative error of at most 0.007.
Values may be sent and summed in bfloat16 or wider, within the bound.
A program may use at most 128 MiB of HBM per device.

```python
import jax
import jax.numpy as jnp
from jax import lax

CH = 256
KBASIS = 9
TAPS = 7
REACH = 6
NLON = 64
SLOTS = 13
NLAT = 256


def support_window(key):
    row_ids = jnp.arange(NLAT, dtype=jnp.int32)
    north_key, south_key = jax.random.split(key)
    north_cut = jax.random.randint(north_key, (NLAT,), 0, 2, dtype=jnp.int32)
    south_cut = jax.random.randint(south_key, (NLAT,), 0, 2, dtype=jnp.int32)
    middle = row_ids == NLAT // 2
    north_cut = jnp.where(middle, 0, jnp.where(row_ids == NLAT - 1, 1, north_cut))
    south_cut = jnp.where(middle, 0, jnp.where(row_ids == 0, 1, south_cut))
    row_first = jnp.maximum(row_ids - (REACH - north_cut), 0)
    row_last = jnp.minimum(row_ids + (REACH - south_cut), NLAT - 1)
    return (row_first, row_last - row_first + 1)


def draw_row_start(key, part):
    return support_window(key)[0]


def draw_row_count(key, part):
    return support_window(key)[1]


def draw_tap_count(key, part):
    key = jax.random.fold_in(key, 7)
    row_ids = jnp.arange(NLAT, dtype=jnp.int32)
    pole_dist = jnp.abs(2 * row_ids - (NLAT - 1))
    jitter = jax.random.randint(key, (NLAT,), 0, 2, dtype=jnp.int32)
    jitter = jnp.where(row_ids == NLAT // 2, 0, jitter)
    half_taps = 1 + (TAPS // 2 - 1) * pole_dist * pole_dist // ((NLAT - 1) * (NLAT - 1)) + jitter
    half_taps = jnp.minimum(half_taps, TAPS // 2)
    return 2 * half_taps + 1


def block_scale(own_key, extent, cuts, least, top_value):
    def one(position, blocks):
        steps = jax.random.uniform(jax.random.fold_in(jax.random.fold_in(own_key, 6), position), (blocks,), jnp.float32, least / len(cuts), top_value / len(cuts))
        return jnp.repeat(jnp.exp(steps), extent[position] // blocks).reshape((-1,) + (1,) * (len(extent) - position - 1))

    gain = one(*cuts[0])
    for cut in cuts[1:]:
        gain = gain * one(*cut)
    return gain


def scatter_about(key, shape, width, reach, cuts=(), held_as=jnp.bfloat16):
    loudness = block_scale(key, shape, cuts, -0.22, 0.18) if cuts else 1.0
    drawn = jax.random.normal(key, shape, jnp.float32) * width * loudness
    return jnp.minimum(jnp.maximum(drawn, -reach), reach).astype(held_as)


def setup_inputs(seed: int = 0, part: int = 0) -> dict:
    keys = jax.random.split(jax.random.key(seed), 8)
    part_splits = jax.random.split(jax.random.fold_in(keys[7], part), 8)
    field = scatter_about(part_splits[0], (NLAT, NLON, CH), 1.0, 6.0, ((0, 16),))
    row_start = draw_row_start(jax.random.fold_in(keys[7], 71), part)
    row_count = draw_row_count(jax.random.fold_in(keys[7], 71), part)
    tap_count = draw_tap_count(jax.random.fold_in(keys[7], 71), part)
    basis = scatter_about(keys[4], (NLAT, SLOTS, TAPS, KBASIS), 0.3, 2.0, ((0, 16),))
    mixing = scatter_about(keys[5], (KBASIS * CH, CH), (KBASIS * CH) ** -0.5, 0.125)
    cotangent = scatter_about(part_splits[6], (NLAT, NLON, CH), 1.0, 6.0, ((0, 16),))
    return {"field": field, "row_start": row_start, "row_count": row_count, "tap_count": tap_count, "basis": basis, "mixing": mixing, "cotangent": cotangent}


def exact_gelu(values):
    return jax.nn.gelu(values, approximate=False)

def reference(field, row_start, row_count, tap_count, basis, mixing, cotangent):
    centre = TAPS // 2
    slot_ids = jnp.arange(SLOTS, dtype=jnp.int32)
    tap_ids = jnp.arange(TAPS, dtype=jnp.int32)
    slot_mask = (slot_ids[None, :] < row_count[:, None]).astype(jnp.float32)
    tap_mask = (jnp.abs(tap_ids - centre)[None, :] <= (tap_count // 2)[:, None]).astype(jnp.float32)
    masked = basis.astype(jnp.float32) * slot_mask[:, :, None, None] * tap_mask[:, None, :, None]
    padded_field = jnp.concatenate([field.astype(jnp.float32), jnp.zeros((SLOTS, NLON, CH), jnp.float32)], axis=0)

    def row_forward(row_item):
        row_first, row_weights = row_item
        window = lax.dynamic_slice(padded_field, (row_first.astype(jnp.int32), jnp.int32(0), jnp.int32(0)), (SLOTS, NLON, CH))
        rolled = jnp.stack([jnp.roll(window, centre - tap_index, axis=1) for tap_index in range(TAPS)])
        summed = jnp.einsum('stk,tsnc->nkc', row_weights, rolled, precision=lax.Precision.HIGHEST)
        return summed.reshape(NLON, KBASIS * CH)
    features = lax.map(row_forward, (row_start, masked)).astype(jnp.bfloat16)
    feature_rows = features.reshape(NLAT * NLON, KBASIS * CH)
    pre_act = jnp.dot(feature_rows, mixing, preferred_element_type=jnp.float32)
    activated, gelu_pull = jax.vjp(exact_gelu, pre_act)
    hidden = activated.astype(jnp.bfloat16).reshape(NLAT, NLON, CH)
    pre_grad = gelu_pull(cotangent.reshape(NLAT * NLON, CH).astype(jnp.float32))[0].astype(jnp.bfloat16)
    feature_grad = lax.dot_general(pre_grad, mixing, (((1,), (1,)), ((), ())), preferred_element_type=jnp.float32).astype(jnp.bfloat16)
    mixing_grad = lax.dot_general(feature_rows, pre_grad, (((0,), (0,)), ((), ())), preferred_element_type=jnp.float32)
    grad_rows = feature_grad.reshape(NLAT, NLON, KBASIS, CH)

    def row_back(row_index, running):
        row_grad = lax.dynamic_index_in_dim(grad_rows, row_index, 0, keepdims=False).astype(jnp.float32)
        rolled = jnp.stack([jnp.roll(row_grad, tap_index - centre, axis=0) for tap_index in range(TAPS)])
        row_weights = lax.dynamic_index_in_dim(masked, row_index, 0, keepdims=False)
        contrib = jnp.einsum('stk,tnkc->snc', row_weights, rolled, precision=lax.Precision.HIGHEST)
        row_first = lax.dynamic_index_in_dim(row_start, row_index, 0, keepdims=False).astype(jnp.int32)
        slice_at = (row_first, jnp.int32(0), jnp.int32(0))
        current = lax.dynamic_slice(running, slice_at, (SLOTS, NLON, CH))
        return lax.dynamic_update_slice(running, current + contrib, slice_at)
    field_sum = lax.fori_loop(0, NLAT, row_back, jnp.zeros((NLAT + SLOTS, NLON, CH), jnp.float32))
    field_grad = field_sum[:NLAT].astype(jnp.bfloat16)
    return (hidden, field_grad, mixing_grad)
```

```python
import jax
import jax.numpy as jnp
from jax import lax
from jax.experimental import pallas as pl
from jax.experimental.pallas import tpu as pltpu
from jax.sharding import PartitionSpec as P

BF16 = jnp.bfloat16
F32 = jnp.float32
TILE = 16


def from_behind(block, axis, distance):
    devices = range(lax.axis_size(axis))
    route = [(i - distance, i) for i in devices if i - distance in devices]
    return lax.ppermute(block, axis, route)


def dot(a, b, dims=((1,), (0,))):
    return lax.dot_general(a, b, (dims, ((), ())), preferred_element_type=F32)


def swap_matrix():
    side = TILE * TILE
    row = lax.broadcasted_iota(jnp.int32, (side, side), 0)
    col = lax.broadcasted_iota(jnp.int32, (side, side), 1)
    return jnp.where((row & (TILE - 1)) * TILE + (row >> 4) == col, 1.0, 0.0).astype(BF16)


def fwd_kernel(dims, field, low, high, wf, mix, cot, hidden, pre_grad, mix_grad, x, feat, halo):
    lon, ch, kb, taps, reach = dims
    centre = taps // 2
    band = 2 * TILE
    blocks = lon // TILE
    side = TILE * TILE
    swap = swap_matrix()
    halo[0:reach] = low[...]
    halo[reach : 2 * reach] = high[...]
    halo[2 * reach :] = jnp.zeros((TILE - 2 * reach, lon, ch), BF16)
    for b in range(blocks):
        at = slice(b * TILE, (b + 1) * TILE)
        own_t = dot(swap, field[:, at, :].reshape(side, ch)).astype(BF16)
        halo_t = dot(swap, halo[:, at, :].reshape(side, ch)).astype(BF16)
        both = jnp.concatenate(
            [own_t.reshape(TILE, TILE, ch), halo_t.reshape(TILE, TILE, ch)], axis=1
        )
        x[(centre + b * TILE) * band : (centre + (b + 1) * TILE) * band, :] = both.reshape(
            TILE * band, ch
        )
    x[0 : centre * band, :] = x[lon * band : (lon + centre) * band, :]
    x[(lon + centre) * band :, :] = x[centre * band : 2 * centre * band, :]

    weights = wf[...]

    @pl.loop(0, lon // 4)
    def _(q):
        for u in range(4):
            n = q * 4 + u
            window = x[pl.ds(pl.multiple_of(n * band, band), taps * band), :]
            f = dot(weights, window).astype(BF16)
            for k in range(kb):
                feat[pl.ds(pl.multiple_of(n * TILE, TILE), TILE), k * ch : (k + 1) * ch] = f[
                    k * TILE : (k + 1) * TILE
                ]

    for b in range(blocks):
        at = slice(b * TILE, (b + 1) * TILE)
        rows = slice(b * side, (b + 1) * side)
        pre = dot(feat[rows, :], mix[...])
        cot_t = dot(swap, cot[:, at, :].reshape(side, ch))
        cdf = 0.5 * (1.0 + lax.erf(pre * (0.5**0.5)))
        pdf = jnp.exp(-0.5 * pre * pre) * 0.3989422804014327
        h = (pre * cdf).astype(BF16)
        hidden[:, at, :] = dot(swap, h).astype(BF16).reshape(TILE, TILE, ch)
        pre_grad[rows, :] = (cot_t * (cdf + pre * pdf)).astype(BF16)
    for k in range(kb):
        cols = slice(k * ch, (k + 1) * ch)
        mix_grad[cols, :] = dot(feat[:, cols], pre_grad[...], ((0,), (0,)))


def bwd_kernel(dims, pre_grad, mix, wb, own, low, high, grads, acc):
    lon, ch, kb, taps, reach = dims
    centre = taps // 2
    band = 2 * TILE
    blocks = lon // TILE
    side = TILE * TILE
    swap = swap_matrix()
    for k in range(kb):
        fg = dot(pre_grad[...], mix[k * ch : (k + 1) * ch, :], ((1,), (1,))).astype(BF16)
        grads[:, k * TILE : (k + 1) * TILE, :] = fg.reshape(lon, TILE, ch)
    acc[...] = jnp.zeros_like(acc)
    weights = wb[...]

    @pl.loop(0, lon // 4)
    def _(q):
        for u in range(4):
            n = q * 4 + u
            at = pl.ds(pl.multiple_of(n * band, band), taps * band)
            acc[at, :] += dot(weights, grads[n])

    acc[lon * band : (lon + centre) * band, :] += acc[0 : centre * band, :]
    acc[centre * band : 2 * centre * band, :] += acc[(lon + centre) * band :, :]
    for b in range(blocks):
        at = slice(b * TILE, (b + 1) * TILE)
        blk = acc[(centre + b * TILE) * band : (centre + (b + 1) * TILE) * band, :]
        blk = blk.reshape(TILE, band, ch)
        mine = blk[:, :TILE, :].reshape(side, ch)
        top = mine.astype(BF16)
        rest = (mine - top.astype(F32)).astype(BF16)
        own[:, at, :] = (dot(swap, top) + dot(swap, rest)).reshape(TILE, TILE, ch)
        near = dot(swap, blk[:, TILE:, :].reshape(side, ch).astype(BF16)).astype(BF16)
        near = near.reshape(TILE, TILE, ch)
        low[:, at, :] = near[:reach]
        high[:, at, :] = near[reach : 2 * reach]


def swap_with(block, step, size, ids):
    route = [(i, ids(i, step)) for i in range(size)]
    return lax.ppermute(block, "lat", route)


def sum_over_bands(partial, shard_rows, channels):
    size = lax.axis_size("lat")
    if size != 16:
        return lax.psum_scatter(partial, "lat", scatter_dimension=0, tiled=True)
    me = lax.axis_index("lat")
    core, row, depth = me & 1, (me >> 1) & 1, me >> 2
    left = partial.reshape(4, 2, 2, shard_rows, channels)

    def take(array, index, axis):
        return lax.dynamic_index_in_dim(array, index, axis, keepdims=False)

    got = swap_with(take(left, 1 - core, 2).astype(BF16), 1, size, lambda i, s: i ^ 1)
    left = take(left, core, 2) + got.astype(F32)
    got = swap_with(take(left, 1 - row, 1).astype(BF16), 1, size, lambda i, s: i ^ 2)
    left = take(left, row, 1) + got.astype(F32)
    total = take(left, depth, 0)
    for step in (1, 2, 3):
        piece = take(left, (depth + step) & 3, 0).astype(BF16)
        got = swap_with(piece, step, size, lambda i, s: (i + 4 * s) % 16)
        total = total + got.astype(F32)
    return total


def local(field, row_start, row_count, tap_count, basis, mixing, cotangent):
    rows_dev, lon, ch = field.shape
    slots, taps, kb = basis.shape[1:]
    reach = (slots - 1) // 2
    band = 2 * TILE
    dims = (lon, ch, kb, taps, reach)
    centre = taps // 2
    low_in = from_behind(field[rows_dev - reach :], "lat", 1)
    high_in = from_behind(field[:reach], "lat", -1)

    first_row = lax.axis_index("lat") * rows_dev - reach
    slot_ids = jnp.arange(slots, dtype=jnp.int32)
    tap_ids = jnp.arange(taps, dtype=jnp.int32)
    at_row = (row_start - first_row)[:, None] + slot_ids[None, :]
    place = jnp.where(
        at_row < reach,
        at_row + TILE,
        jnp.where(at_row < reach + rows_dev, at_row - reach, at_row),
    )
    placing = (place[:, :, None] == jnp.arange(band, dtype=jnp.int32)) & (
        slot_ids[None, :] < row_count[:, None]
    )[:, :, None]
    tap_mask = jnp.abs(tap_ids - centre)[None, :] <= (tap_count // 2)[:, None]
    masked = jnp.where(tap_mask[:, None, :, None], basis, jnp.zeros((), BF16))
    placed = lax.dot_general(
        masked.reshape(rows_dev, slots, taps * kb),
        placing.astype(BF16),
        (((1,), (1,)), ((0,), (0,))),
        preferred_element_type=F32,
    ).astype(BF16)
    placed = placed.reshape(rows_dev, taps, kb, band)
    wf = placed.transpose(2, 0, 1, 3).reshape(kb * rows_dev, taps * band)
    wb = wf.T

    rows = rows_dev * lon
    vmem = pl.BlockSpec(memory_space=pltpu.VMEM)
    hidden, pre_grad, mix_part = pl.pallas_call(
        lambda *refs: fwd_kernel(dims, *refs),
        out_shape=(
            jax.ShapeDtypeStruct((rows_dev, lon, ch), BF16),
            jax.ShapeDtypeStruct((rows, ch), BF16),
            jax.ShapeDtypeStruct((kb * ch, ch), F32),
        ),
        in_specs=[vmem] * 6,
        out_specs=(vmem,) * 3,
        scratch_shapes=[
            pltpu.VMEM(((lon + taps - 1) * band, ch), BF16),
            pltpu.VMEM((rows, kb * ch), BF16),
            pltpu.VMEM((TILE, lon, ch), BF16),
        ],
        compiler_params=pltpu.CompilerParams(vmem_limit_bytes=40 * 2**20),
        cost_estimate=pl.CostEstimate(
            flops=6 * rows * kb * ch * ch, bytes_accessed=8 * 2**20, transcendentals=2 * rows * ch
        ),
        name="features_hidden_mixing_grad",
    )(field, low_in, high_in, wf, mixing, cotangent)

    own, low, high = pl.pallas_call(
        lambda *refs: bwd_kernel(dims, *refs),
        out_shape=(
            jax.ShapeDtypeStruct((rows_dev, lon, ch), F32),
            jax.ShapeDtypeStruct((reach, lon, ch), BF16),
            jax.ShapeDtypeStruct((reach, lon, ch), BF16),
        ),
        in_specs=[vmem] * 3,
        out_specs=(vmem,) * 3,
        scratch_shapes=[
            pltpu.VMEM((lon, kb * TILE, ch), BF16),
            pltpu.VMEM(((lon + taps - 1) * band, ch), F32),
        ],
        compiler_params=pltpu.CompilerParams(vmem_limit_bytes=40 * 2**20),
        cost_estimate=pl.CostEstimate(
            flops=4 * rows * kb * ch * ch, bytes_accessed=8 * 2**20, transcendentals=0
        ),
        name="field_grad_of_band",
    )(pre_grad, mixing, wb)

    mixing_grad = sum_over_bands(mix_part, kb * ch // lax.axis_size("lat"), ch)
    from_high = from_behind(low, "lat", -1).astype(F32)
    from_low = from_behind(high, "lat", 1).astype(F32)
    filler = jnp.zeros((rows_dev - reach, lon, ch), F32)
    field_grad = (
        own
        + jnp.concatenate([filler, from_high], axis=0)
        + jnp.concatenate([from_low, filler], axis=0)
    ).astype(BF16)
    return (hidden, field_grad, mixing_grad)


def solution(mesh):
    placed = (
        P(("member", "lat"), None, None),
        P("lat"),
        P("lat"),
        P("lat"),
        P("lat", None, None, None),
        P(),
        P(("member", "lat"), None, None),
    )
    return jax.shard_map(
        local,
        mesh=mesh,
        in_specs=placed,
        out_specs=(
            P(("member", "lat"), None, None),
            P(("member", "lat"), None, None),
            P(("member", "lat"), None),
        ),
        check_vma=False,
    )
```

```python
import jax
import jax.numpy as jnp
from jax import lax
from jax.experimental import pallas as pl
from jax.experimental.pallas import tpu as pltpu
from jax.sharding import PartitionSpec as P

BF16 = jnp.bfloat16
F32 = jnp.float32
TILE = 16


def from_behind(block, axis, distance):
    devices = range(lax.axis_size(axis))
    route = [(i - distance, i) for i in devices if i - distance in devices]
    return lax.ppermute(block, axis, route)


def dot(a, b, dims=((1,), (0,))):
    return lax.dot_general(a, b, (dims, ((), ())), preferred_element_type=F32)


def swap_matrix():
    side = TILE * TILE
    row = lax.broadcasted_iota(jnp.int32, (side, side), 0)
    col = lax.broadcasted_iota(jnp.int32, (side, side), 1)
    return jnp.where((row & (TILE - 1)) * TILE + (row >> 4) == col, 1.0, 0.0).astype(BF16)


def fwd_kernel(dims, field, low, high, wf, mix, cot, hidden, pre_grad, mix_grad, x, feat, halo):
    lon, ch, kb, taps, reach = dims
    centre = taps // 2
    band = 2 * TILE
    blocks = lon // TILE
    side = TILE * TILE
    swap = swap_matrix()
    halo[0:reach] = low[...]
    halo[reach : 2 * reach] = high[...]
    halo[2 * reach :] = jnp.zeros((TILE - 2 * reach, lon, ch), BF16)
    for b in range(blocks):
        at = slice(b * TILE, (b + 1) * TILE)
        own_t = dot(swap, field[:, at, :].reshape(side, ch)).astype(BF16)
        halo_t = dot(swap, halo[:, at, :].reshape(side, ch)).astype(BF16)
        both = jnp.concatenate(
            [own_t.reshape(TILE, TILE, ch), halo_t.reshape(TILE, TILE, ch)], axis=1
        )
        x[(centre + b * TILE) * band : (centre + (b + 1) * TILE) * band, :] = both.reshape(
            TILE * band, ch
        )
    x[0 : centre * band, :] = x[lon * band : (lon + centre) * band, :]
    x[(lon + centre) * band :, :] = x[centre * band : 2 * centre * band, :]

    weights = wf[...]

    @pl.loop(0, lon // 4)
    def _(q):
        for u in range(4):
            n = q * 4 + u
            window = x[pl.ds(pl.multiple_of(n * band, band), taps * band), :]
            f = dot(weights, window).astype(BF16)
            for k in range(kb):
                feat[pl.ds(pl.multiple_of(n * TILE, TILE), TILE), k * ch : (k + 1) * ch] = f[
                    k * TILE : (k + 1) * TILE
                ]

    for b in range(blocks):
        at = slice(b * TILE, (b + 1) * TILE)
        rows = slice(b * side, (b + 1) * side)
        pre = dot(feat[rows, :], mix[...])
        cot_t = dot(swap, cot[:, at, :].reshape(side, ch))
        cdf = 0.5 * (1.0 + lax.erf(pre * (0.5**0.5)))
        pdf = jnp.exp(-0.5 * pre * pre) * 0.3989422804014327
        h = (pre * cdf).astype(BF16)
        hidden[:, at, :] = dot(swap, h).astype(BF16).reshape(TILE, TILE, ch)
        pre_grad[rows, :] = (cot_t * (cdf + pre * pdf)).astype(BF16)
    for k in range(kb):
        cols = slice(k * ch, (k + 1) * ch)
        mix_grad[cols, :] = dot(feat[:, cols], pre_grad[...], ((0,), (0,)))


def bwd_kernel(dims, pre_grad, mix, wb, own, low, high, grads, acc):
    lon, ch, kb, taps, reach = dims
    centre = taps // 2
    band = 2 * TILE
    blocks = lon // TILE
    side = TILE * TILE
    swap = swap_matrix()
    for k in range(kb):
        fg = dot(pre_grad[...], mix[k * ch : (k + 1) * ch, :], ((1,), (1,))).astype(BF16)
        grads[:, k * TILE : (k + 1) * TILE, :] = fg.reshape(lon, TILE, ch)
    acc[...] = jnp.zeros_like(acc)
    weights = wb[...]

    @pl.loop(0, lon // 4)
    def _(q):
        for u in range(4):
            n = q * 4 + u
            at = pl.ds(pl.multiple_of(n * band, band), taps * band)
            acc[at, :] += dot(weights, grads[n])

    acc[lon * band : (lon + centre) * band, :] += acc[0 : centre * band, :]
    acc[centre * band : 2 * centre * band, :] += acc[(lon + centre) * band :, :]
    for b in range(blocks):
        at = slice(b * TILE, (b + 1) * TILE)
        blk = acc[(centre + b * TILE) * band : (centre + (b + 1) * TILE) * band, :]
        blk = blk.reshape(TILE, band, ch)
        mine = blk[:, :TILE, :].reshape(side, ch)
        top = mine.astype(BF16)
        rest = (mine - top.astype(F32)).astype(BF16)
        own[:, at, :] = (dot(swap, top) + dot(swap, rest)).reshape(TILE, TILE, ch)
        near = dot(swap, blk[:, TILE:, :].reshape(side, ch).astype(BF16)).astype(BF16)
        near = near.reshape(TILE, TILE, ch)
        low[:, at, :] = near[:reach]
        high[:, at, :] = near[reach : 2 * reach]


def remote(src, dst, send, recv, target):
    return pltpu.make_async_remote_copy(
        src_ref=src,
        dst_ref=dst,
        send_sem=send,
        recv_sem=recv,
        device_id={"lat": target},
        device_id_type=pl.DeviceIdType.MESH,
    )


def fused_kernel(
    dims, field_in, wf, wb, mix_in, cot_in, hidden, field_grad, mix_shard,
    field, mix, cot, halo, x, feat, pre_grad, mix_grad, grads, acc, own,
    near, got, c_out, c_in, y_out, y_in, z_out, z_in, kept,
    l_sem, f_send, f_recv, b_send, b_recv, c_send, c_recv, y_send, y_recv, z_send, z_recv,
):
    lon, ch, kb, taps, reach = dims
    centre = taps // 2
    band = 2 * TILE
    blocks = lon // TILE
    side = TILE * TILE
    rows_dev = field.shape[0]
    shard = mix_shard.shape[0]
    me = lax.axis_index("lat")
    last = lax.axis_size("lat") - 1
    core = me % 2
    row = (me // 2) % 2
    depth = me // 4
    other_core = me + 1 - 2 * core
    other_row = me + 2 - 4 * row
    far = me - 1 + 2 * core
    has_far = (far >= 0) & (far <= last)
    has_low = me > 0
    has_high = me < last

    loads = [
        pltpu.make_async_copy(src, dst, l_sem.at[i])
        for i, (src, dst) in enumerate(((field_in, field), (cot_in, cot), (mix_in, mix)))
    ]
    for load in loads:
        load.start()

    barrier = pltpu.get_barrier_semaphore()

    def greet(device):
        pl.semaphore_signal(
            barrier, inc=1, device_id={"lat": device}, device_id_type=pl.DeviceIdType.MESH
        )

    greet(other_core)
    greet(other_row)
    for step in (1, 2, 3):
        greet((me + 4 * step) % 16)

    @pl.when(has_far)
    def _():
        greet(far)

    pl.semaphore_wait(barrier, 5 + has_far.astype(jnp.int32))

    up = remote(
        field_in.at[rows_dev - reach : rows_dev], halo.at[0:reach], f_send.at[0], f_recv.at[0],
        me + 1,
    )
    down = remote(
        field_in.at[0:reach], halo.at[reach : 2 * reach], f_send.at[1], f_recv.at[1],
        me - 1,
    )

    @pl.when(has_high)
    def _():
        up.start()

    @pl.when(has_low)
    def _():
        down.start()

    none = jnp.zeros((reach, lon, ch), BF16)

    @pl.when(me == 0)
    def _():
        halo[0:reach] = none
        got[0:reach] = none

    @pl.when(me == last)
    def _():
        halo[reach : 2 * reach] = none
        got[reach : 2 * reach] = none

    halo[2 * reach :] = jnp.zeros((TILE - 2 * reach, lon, ch), BF16)
    swap = swap_matrix()
    loads[0].wait()
    for b in range(blocks):
        at = slice(b * TILE, (b + 1) * TILE)
        to = slice(centre + b * TILE, centre + (b + 1) * TILE)
        part = dot(swap, field[:, at, :].reshape(side, ch)).astype(BF16)
        x[to, 0:TILE, :] = part.reshape(TILE, TILE, ch)
    loads[1].wait()
    loads[2].wait()

    @pl.when(has_low)
    def _():
        up.wait_recv()

    @pl.when(has_high)
    def _():
        down.wait_recv()

    for b in range(blocks):
        at = slice(b * TILE, (b + 1) * TILE)
        to = slice(centre + b * TILE, centre + (b + 1) * TILE)
        part = dot(swap, halo[:, at, :].reshape(side, ch)).astype(BF16)
        x[to, TILE:band, :] = part.reshape(TILE, TILE, ch)
    x[0:centre] = x[lon : lon + centre]
    x[lon + centre :] = x[centre : 2 * centre]

    weights = wf[...]

    @pl.loop(0, lon // 4)
    def _(q):
        for u in range(4):
            n = q * 4 + u
            window = x[pl.ds(n, taps)].reshape(taps * band, ch)
            f = dot(weights, window).astype(BF16)
            for k in range(kb):
                feat[pl.ds(pl.multiple_of(n * TILE, TILE), TILE), k * ch : (k + 1) * ch] = f[
                    k * TILE : (k + 1) * TILE
                ]

    for b in range(blocks):
        at = slice(b * TILE, (b + 1) * TILE)
        rows = slice(b * side, (b + 1) * side)
        pre = dot(feat[rows, :], mix[...])
        cot_t = dot(swap, cot[:, at, :].reshape(side, ch))
        cdf = 0.5 * (1.0 + lax.erf(pre * (0.5**0.5)))
        pdf = jnp.exp(-0.5 * pre * pre) * 0.3989422804014327
        h = (pre * cdf).astype(BF16)
        hidden[:, at, :] = dot(swap, h).astype(BF16).reshape(TILE, TILE, ch)
        pre_grad[rows, :] = (cot_t * (cdf + pre * pdf)).astype(BF16)

    def term(z, y, c):
        first = pl.multiple_of((4 * z + 2 * y + c) * shard, TILE)
        return mix_grad[pl.ds(first, shard), :]

    def by_core(z):
        return remote(c_out.at[z], c_in.at[z], c_send.at[z], c_recv.at[z], other_core)

    def by_row(z):
        return remote(y_out.at[z], y_in.at[z], y_send.at[z], y_recv.at[z], other_row)

    def by_depth(z):
        slot = (depth + 7 - z) % 4
        return remote(
            z_out.at[z], z_in.at[slot], z_send.at[z], z_recv.at[slot], 4 * z + me % 4
        )

    def send_core(z):
        for y in range(2):
            c_out[z, y] = term(z, y, 1 - core).astype(BF16)
        by_core(z).start()

    def send_row(z):
        by_core(z).wait_recv()
        y_out[z] = (term(z, 1 - row, core) + c_in[z, 1 - row].astype(F32)).astype(BF16)
        by_row(z).start()

    def send_depth(z):
        by_row(z).wait_recv()
        total = term(z, row, core) + c_in[z, row].astype(F32) + y_in[z].astype(F32)

        @pl.when(depth == z)
        def _():
            kept[...] = total

        @pl.when(depth != z)
        def _():
            z_out[z] = total.astype(BF16)
            by_depth(z).start()

    for k in range(kb):
        cols = slice(k * ch, (k + 1) * ch)
        mix_grad[cols, :] = dot(feat[:, cols], pre_grad[...], ((0,), (0,)))
        done = (k + 1) * ch // (4 * shard) - 1
        before = k * ch // (4 * shard) - 1
        if done > before:
            send_core(done)
            if done > 0:
                send_row(done - 1)

    for k in range(kb):
        fg = dot(pre_grad[...], mix[k * ch : (k + 1) * ch, :], ((1,), (1,))).astype(BF16)
        grads[:, k * TILE : (k + 1) * TILE, :] = fg.reshape(lon, TILE, ch)
        if k == 1:
            send_row(3)
        if k == 3:
            send_depth(0)
        if k == 6:
            send_depth(1)
    acc[...] = jnp.zeros_like(acc)
    back = wb[...]

    def spread(q):
        for u in range(4):
            n = q * 4 + u
            at = pl.ds(pl.multiple_of(n * band, band), taps * band)
            acc[at, :] += dot(back, grads[n])

    pl.loop(0, lon // 8)(spread)
    send_depth(2)
    pl.loop(lon // 8, lon // 4)(spread)
    send_depth(3)

    acc[lon * band : (lon + centre) * band, :] += acc[0 : centre * band, :]
    acc[centre * band : 2 * centre * band, :] += acc[(lon + centre) * band :, :]

    def block_of(b):
        blk = acc[(centre + b * TILE) * band : (centre + (b + 1) * TILE) * band, :]
        return blk.reshape(TILE, band, ch)

    for b in range(blocks):
        part = block_of(b)[:, TILE:, :].reshape(side, ch).astype(BF16)
        near[:, b * TILE : (b + 1) * TILE, :] = dot(swap, part).astype(BF16).reshape(TILE, TILE, ch)
    to_low = remote(
        near.at[0:reach], got.at[reach : 2 * reach], b_send.at[0], b_recv.at[0],
        me - 1,
    )
    to_high = remote(
        near.at[reach : 2 * reach], got.at[0:reach], b_send.at[1], b_recv.at[1],
        me + 1,
    )

    @pl.when(has_low)
    def _():
        to_low.start()

    @pl.when(has_high)
    def _():
        to_high.start()

    for b in range(blocks):
        mine = block_of(b)[:, :TILE, :].reshape(side, ch)
        top = mine.astype(BF16)
        rest = (mine - top.astype(F32)).astype(BF16)
        own[:, b * TILE : (b + 1) * TILE, :] = (dot(swap, top) + dot(swap, rest)).reshape(
            TILE, TILE, ch
        )
    field_grad[reach : rows_dev - reach] = own[reach : rows_dev - reach].astype(BF16)

    @pl.when(has_high)
    def _():
        to_low.wait_recv()

    field_grad[rows_dev - reach :] = (
        own[rows_dev - reach :] + got[reach : 2 * reach].astype(F32)
    ).astype(BF16)

    @pl.when(has_low)
    def _():
        to_high.wait_recv()

    field_grad[0:reach] = (own[0:reach] + got[0:reach].astype(F32)).astype(BF16)

    total = kept[...]
    for slot in range(3):
        remote(
            z_out.at[0], z_in.at[slot], z_send.at[0], z_recv.at[slot], other_row
        ).wait_recv()
        total = total + z_in[slot].astype(F32)
    mix_shard[...] = total

    @pl.when(has_high)
    def _():
        up.wait_send()
        to_high.wait_send()

    @pl.when(has_low)
    def _():
        down.wait_send()
        to_low.wait_send()

    for z in range(4):
        by_core(z).wait_send()
        by_row(z).wait_send()

        @pl.when(depth != z)
        def _():
            by_depth(z).wait_send()


def fused(dims, field, wf, wb, mixing, cotangent):
    lon, ch, kb, taps, reach = dims
    rows_dev = field.shape[0]
    rows = rows_dev * lon
    shard = kb * ch // 16
    vmem = pl.BlockSpec(memory_space=pltpu.VMEM)
    hbm = pl.BlockSpec(memory_space=pl.ANY)
    band = 2 * TILE
    sems = pltpu.SemaphoreType.DMA
    return pl.pallas_call(
        lambda *refs: fused_kernel(dims, *refs),
        out_shape=(
            jax.ShapeDtypeStruct((rows_dev, lon, ch), BF16),
            jax.ShapeDtypeStruct((rows_dev, lon, ch), BF16),
            jax.ShapeDtypeStruct((shard, ch), F32),
        ),
        in_specs=[hbm, vmem, vmem, hbm, hbm],
        out_specs=(vmem,) * 3,
        scratch_shapes=[
            pltpu.VMEM((rows_dev, lon, ch), BF16),
            pltpu.VMEM((kb * ch, ch), BF16),
            pltpu.VMEM((rows_dev, lon, ch), BF16),
            pltpu.VMEM((TILE, lon, ch), BF16),
            pltpu.VMEM((lon + taps - 1, band, ch), BF16),
            pltpu.VMEM((rows, kb * ch), BF16),
            pltpu.VMEM((rows, ch), BF16),
            pltpu.VMEM((kb * ch, ch), F32),
            pltpu.VMEM((lon, kb * TILE, ch), BF16),
            pltpu.VMEM(((lon + taps - 1) * band, ch), F32),
            pltpu.VMEM((rows_dev, lon, ch), F32),
            pltpu.VMEM((TILE, lon, ch), BF16),
            pltpu.VMEM((2 * reach, lon, ch), BF16),
            pltpu.VMEM((4, 2, shard, ch), BF16),
            pltpu.VMEM((4, 2, shard, ch), BF16),
            pltpu.VMEM((4, shard, ch), BF16),
            pltpu.VMEM((4, shard, ch), BF16),
            pltpu.VMEM((4, shard, ch), BF16),
            pltpu.VMEM((3, shard, ch), BF16),
            pltpu.VMEM((shard, ch), F32),
            sems((3,)), sems((2,)), sems((2,)), sems((2,)), sems((2,)), sems((4,)),
            sems((4,)), sems((4,)), sems((4,)), sems((4,)), sems((3,)),
        ],
        compiler_params=pltpu.CompilerParams(
            vmem_limit_bytes=48 * 2**20, collective_id=0, has_side_effects=True
        ),
        cost_estimate=pl.CostEstimate(
            flops=10 * rows * kb * ch * ch, bytes_accessed=8 * 2**20, transcendentals=2 * rows * ch
        ),
        name="conv_and_gradients",
    )(field, wf, wb, mixing, cotangent)


def local(field, row_start, row_count, tap_count, basis, mixing, cotangent):
    rows_dev, lon, ch = field.shape
    slots, taps, kb = basis.shape[1:]
    reach = (slots - 1) // 2
    band = 2 * TILE
    dims = (lon, ch, kb, taps, reach)
    centre = taps // 2

    first_row = lax.axis_index("lat") * rows_dev - reach
    slot_ids = jnp.arange(slots, dtype=jnp.int32)
    tap_ids = jnp.arange(taps, dtype=jnp.int32)
    at_row = (row_start - first_row)[:, None] + slot_ids[None, :]
    place = jnp.where(
        at_row < reach,
        at_row + TILE,
        jnp.where(at_row < reach + rows_dev, at_row - reach, at_row),
    )
    placing = (place[:, :, None] == jnp.arange(band, dtype=jnp.int32)) & (
        slot_ids[None, :] < row_count[:, None]
    )[:, :, None]
    tap_mask = jnp.abs(tap_ids - centre)[None, :] <= (tap_count // 2)[:, None]
    masked = jnp.where(tap_mask[:, None, :, None], basis, jnp.zeros((), BF16))
    placed = lax.dot_general(
        masked.reshape(rows_dev, slots, taps * kb),
        placing.astype(BF16),
        (((1,), (1,)), ((0,), (0,))),
        preferred_element_type=F32,
    ).astype(BF16)
    placed = placed.reshape(rows_dev, taps, kb, band)
    wf = placed.transpose(2, 0, 1, 3).reshape(kb * rows_dev, taps * band)
    wb = wf.T

    if lax.axis_size("lat") == 16:
        return fused(dims, field, wf, wb, mixing, cotangent)

    low_in = from_behind(field[rows_dev - reach :], "lat", 1)
    high_in = from_behind(field[:reach], "lat", -1)
    rows = rows_dev * lon
    vmem = pl.BlockSpec(memory_space=pltpu.VMEM)
    hidden, pre_grad, mix_part = pl.pallas_call(
        lambda *refs: fwd_kernel(dims, *refs),
        out_shape=(
            jax.ShapeDtypeStruct((rows_dev, lon, ch), BF16),
            jax.ShapeDtypeStruct((rows, ch), BF16),
            jax.ShapeDtypeStruct((kb * ch, ch), F32),
        ),
        in_specs=[vmem] * 6,
        out_specs=(vmem,) * 3,
        scratch_shapes=[
            pltpu.VMEM(((lon + taps - 1) * band, ch), BF16),
            pltpu.VMEM((rows, kb * ch), BF16),
            pltpu.VMEM((TILE, lon, ch), BF16),
        ],
        compiler_params=pltpu.CompilerParams(vmem_limit_bytes=40 * 2**20),
        cost_estimate=pl.CostEstimate(
            flops=6 * rows * kb * ch * ch, bytes_accessed=8 * 2**20, transcendentals=2 * rows * ch
        ),
        name="features_hidden_mixing_grad",
    )(field, low_in, high_in, wf, mixing, cotangent)

    own, low, high = pl.pallas_call(
        lambda *refs: bwd_kernel(dims, *refs),
        out_shape=(
            jax.ShapeDtypeStruct((rows_dev, lon, ch), F32),
            jax.ShapeDtypeStruct((reach, lon, ch), BF16),
            jax.ShapeDtypeStruct((reach, lon, ch), BF16),
        ),
        in_specs=[vmem] * 3,
        out_specs=(vmem,) * 3,
        scratch_shapes=[
            pltpu.VMEM((lon, kb * TILE, ch), BF16),
            pltpu.VMEM(((lon + taps - 1) * band, ch), F32),
        ],
        compiler_params=pltpu.CompilerParams(vmem_limit_bytes=40 * 2**20),
        cost_estimate=pl.CostEstimate(
            flops=4 * rows * kb * ch * ch, bytes_accessed=8 * 2**20, transcendentals=0
        ),
        name="field_grad_of_band",
    )(pre_grad, mixing, wb)

    mixing_grad = lax.psum_scatter(mix_part, "lat", scatter_dimension=0, tiled=True)
    from_high = from_behind(low, "lat", -1).astype(F32)
    from_low = from_behind(high, "lat", 1).astype(F32)
    filler = jnp.zeros((rows_dev - reach, lon, ch), F32)
    field_grad = (
        own
        + jnp.concatenate([filler, from_high], axis=0)
        + jnp.concatenate([from_low, filler], axis=0)
    ).astype(BF16)
    return (hidden, field_grad, mixing_grad)


def solution(mesh):
    placed = (
        P(("member", "lat"), None, None),
        P("lat"),
        P("lat"),
        P("lat"),
        P("lat", None, None, None),
        P(),
        P(("member", "lat"), None, None),
    )
    return jax.shard_map(
        local,
        mesh=mesh,
        in_specs=placed,
        out_specs=(
            P(("member", "lat"), None, None),
            P(("member", "lat"), None, None),
            P(("member", "lat"), None),
        ),
        check_vma=False,
    )
```

```python
import jax
import jax.numpy as jnp
from jax import lax
from jax.experimental import pallas as pl
from jax.experimental.pallas import tpu as pltpu
from jax.sharding import PartitionSpec as P

BF16 = jnp.bfloat16
F32 = jnp.float32
TILE = 16


def from_behind(block, axis, distance):
    devices = range(lax.axis_size(axis))
    route = [(i - distance, i) for i in devices if i - distance in devices]
    return lax.ppermute(block, axis, route)


def dot(a, b, dims=((1,), (0,))):
    return lax.dot_general(a, b, (dims, ((), ())), preferred_element_type=F32)


def swap_matrix():
    side = TILE * TILE
    row = lax.broadcasted_iota(jnp.int32, (side, side), 0)
    col = lax.broadcasted_iota(jnp.int32, (side, side), 1)
    return jnp.where((row & (TILE - 1)) * TILE + (row >> 4) == col, 1.0, 0.0).astype(BF16)


def fwd_kernel(dims, field, low, high, wf, mix, cot, hidden, pre_grad, mix_grad, x, feat, halo):
    lon, ch, kb, taps, reach = dims
    centre = taps // 2
    band = 2 * TILE
    blocks = lon // TILE
    side = TILE * TILE
    swap = swap_matrix()
    halo[0:reach] = low[...]
    halo[reach : 2 * reach] = high[...]
    halo[2 * reach :] = jnp.zeros((TILE - 2 * reach, lon, ch), BF16)
    for b in range(blocks):
        at = slice(b * TILE, (b + 1) * TILE)
        own_t = dot(swap, field[:, at, :].reshape(side, ch)).astype(BF16)
        halo_t = dot(swap, halo[:, at, :].reshape(side, ch)).astype(BF16)
        both = jnp.concatenate(
            [own_t.reshape(TILE, TILE, ch), halo_t.reshape(TILE, TILE, ch)], axis=1
        )
        x[(centre + b * TILE) * band : (centre + (b + 1) * TILE) * band, :] = both.reshape(
            TILE * band, ch
        )
    x[0 : centre * band, :] = x[lon * band : (lon + centre) * band, :]
    x[(lon + centre) * band :, :] = x[centre * band : 2 * centre * band, :]

    weights = wf[...]

    @pl.loop(0, lon // 4)
    def _(q):
        for u in range(4):
            n = q * 4 + u
            window = x[pl.ds(pl.multiple_of(n * band, band), taps * band), :]
            f = dot(weights, window).astype(BF16)
            for k in range(kb):
                feat[pl.ds(pl.multiple_of(n * TILE, TILE), TILE), k * ch : (k + 1) * ch] = f[
                    k * TILE : (k + 1) * TILE
                ]

    for b in range(blocks):
        at = slice(b * TILE, (b + 1) * TILE)
        rows = slice(b * side, (b + 1) * side)
        pre = dot(feat[rows, :], mix[...])
        cot_t = dot(swap, cot[:, at, :].reshape(side, ch))
        cdf = 0.5 * (1.0 + lax.erf(pre * (0.5**0.5)))
        pdf = jnp.exp(-0.5 * pre * pre) * 0.3989422804014327
        h = (pre * cdf).astype(BF16)
        hidden[:, at, :] = dot(swap, h).astype(BF16).reshape(TILE, TILE, ch)
        pre_grad[rows, :] = (cot_t * (cdf + pre * pdf)).astype(BF16)
    for k in range(kb):
        cols = slice(k * ch, (k + 1) * ch)
        mix_grad[cols, :] = dot(feat[:, cols], pre_grad[...], ((0,), (0,)))


def bwd_kernel(dims, pre_grad, mix, wb, own, low, high, grads, acc):
    lon, ch, kb, taps, reach = dims
    centre = taps // 2
    band = 2 * TILE
    blocks = lon // TILE
    side = TILE * TILE
    swap = swap_matrix()
    for k in range(kb):
        fg = dot(pre_grad[...], mix[k * ch : (k + 1) * ch, :], ((1,), (1,))).astype(BF16)
        grads[:, k * TILE : (k + 1) * TILE, :] = fg.reshape(lon, TILE, ch)
    acc[...] = jnp.zeros_like(acc)
    weights = wb[...]

    @pl.loop(0, lon // 4)
    def _(q):
        for u in range(4):
            n = q * 4 + u
            at = pl.ds(pl.multiple_of(n * band, band), taps * band)
            acc[at, :] += dot(weights, grads[n])

    acc[lon * band : (lon + centre) * band, :] += acc[0 : centre * band, :]
    acc[centre * band : 2 * centre * band, :] += acc[(lon + centre) * band :, :]
    for b in range(blocks):
        at = slice(b * TILE, (b + 1) * TILE)
        blk = acc[(centre + b * TILE) * band : (centre + (b + 1) * TILE) * band, :]
        blk = blk.reshape(TILE, band, ch)
        mine = blk[:, :TILE, :].reshape(side, ch)
        top = mine.astype(BF16)
        rest = (mine - top.astype(F32)).astype(BF16)
        own[:, at, :] = (dot(swap, top) + dot(swap, rest)).reshape(TILE, TILE, ch)
        near = dot(swap, blk[:, TILE:, :].reshape(side, ch).astype(BF16)).astype(BF16)
        near = near.reshape(TILE, TILE, ch)
        low[:, at, :] = near[:reach]
        high[:, at, :] = near[reach : 2 * reach]


def filter_matrix(dims, basis, start, count, tap_count, first_row):
    lon, ch, kb, taps, reach = dims
    slots = basis.shape[0]
    band = 2 * TILE
    lanes = taps * band
    out_row = lax.broadcasted_iota(jnp.int32, (TILE, lanes), 0)
    lane = lax.broadcasted_iota(jnp.int32, (TILE, lanes), 1)
    place = lane & (band - 1)
    tap = lane >> 5
    in_row = jnp.where(
        place < TILE, place + reach, jnp.where(place < TILE + reach, place - TILE, place)
    )
    first = jnp.zeros((TILE, lanes), jnp.int32)
    used = first
    half = first
    for o in range(TILE):
        here = out_row == o
        first = jnp.where(here, start[o] - first_row, first)
        used = jnp.where(here, count[o], used)
        half = jnp.where(here, tap_count[o] >> 1, half)
    slot = in_row - first
    inside = (slot < used) & (jnp.abs(tap - taps // 2) <= half) & (place < TILE + 2 * reach)
    slot = jnp.where(inside, slot, -1)
    slot = jnp.concatenate([slot] * kb, axis=0)
    to_lane = lax.broadcasted_iota(jnp.int32, (taps, lanes), 1) >> 5
    spread = jnp.where(
        lax.broadcasted_iota(jnp.int32, (taps, lanes), 0) == to_lane, 1.0, 0.0
    ).astype(BF16)
    total = jnp.zeros((kb * TILE, lanes), F32)
    for j in range(slots):
        total = jnp.where(slot == j, dot(basis[j], spread), total)
    return total.astype(BF16)


def remote(src, dst, send, recv, target):
    return pltpu.make_async_remote_copy(
        src_ref=src,
        dst_ref=dst,
        send_sem=send,
        recv_sem=recv,
        device_id={"lat": target},
        device_id_type=pl.DeviceIdType.MESH,
    )


def fused_kernel(
    dims, field_in, basis, start, count, tap_count, mix_in, cot_in, hidden, field_grad, mix_shard,
    wf, wb, field, mix, cot, halo, x, feat, pre_grad, mix_grad, grads, acc, own,
    near, got, c_out, c_in, y_out, y_in, z_out, z_in, kept,
    l_sem, f_send, f_recv, b_send, b_recv, c_send, c_recv, y_send, y_recv, z_send, z_recv,
):
    lon, ch, kb, taps, reach = dims
    centre = taps // 2
    band = 2 * TILE
    blocks = lon // TILE
    side = TILE * TILE
    rows_dev = field.shape[0]
    shard = mix_shard.shape[0]
    me = lax.axis_index("lat")
    last = lax.axis_size("lat") - 1
    core = me % 2
    row = (me // 2) % 2
    depth = me // 4
    other_core = me + 1 - 2 * core
    other_row = me + 2 - 4 * row
    far = me - 1 + 2 * core
    has_far = (far >= 0) & (far <= last)
    has_low = me > 0
    has_high = me < last

    loads = [
        pltpu.make_async_copy(src, dst, l_sem.at[i])
        for i, (src, dst) in enumerate(((field_in, field), (cot_in, cot), (mix_in, mix)))
    ]
    for load in loads:
        load.start()

    barrier = pltpu.get_barrier_semaphore()

    def greet(device):
        pl.semaphore_signal(
            barrier, inc=1, device_id={"lat": device}, device_id_type=pl.DeviceIdType.MESH
        )

    greet(other_core)
    greet(other_row)
    for step in (1, 2, 3):
        greet((me + 4 * step) % 16)

    @pl.when(has_far)
    def _():
        greet(far)

    pl.semaphore_wait(barrier, 5 + has_far.astype(jnp.int32))

    up = remote(
        field_in.at[rows_dev - reach : rows_dev], halo.at[0:reach], f_send.at[0], f_recv.at[0],
        me + 1,
    )
    down = remote(
        field_in.at[0:reach], halo.at[reach : 2 * reach], f_send.at[1], f_recv.at[1],
        me - 1,
    )

    @pl.when(has_high)
    def _():
        up.start()

    @pl.when(has_low)
    def _():
        down.start()

    none = jnp.zeros((reach, lon, ch), BF16)

    @pl.when(me == 0)
    def _():
        halo[0:reach] = none
        got[0:reach] = none

    @pl.when(me == last)
    def _():
        halo[reach : 2 * reach] = none
        got[reach : 2 * reach] = none

    halo[2 * reach :] = jnp.zeros((TILE - 2 * reach, lon, ch), BF16)
    swap = swap_matrix()
    loads[0].wait()
    for b in range(blocks):
        at = slice(b * TILE, (b + 1) * TILE)
        to = slice(centre + b * TILE, centre + (b + 1) * TILE)
        part = dot(swap, field[:, at, :].reshape(side, ch)).astype(BF16)
        x[to, 0:TILE, :] = part.reshape(TILE, TILE, ch)
    wf[...] = filter_matrix(dims, basis, start, count, tap_count, me * rows_dev - reach)
    side_k = kb * TILE
    eye = jnp.where(
        lax.broadcasted_iota(jnp.int32, (side_k, side_k), 0)
        == lax.broadcasted_iota(jnp.int32, (side_k, side_k), 1),
        1.0,
        0.0,
    ).astype(BF16)
    wb[...] = dot(wf[...], eye, ((0,), (0,))).astype(BF16)
    loads[1].wait()
    loads[2].wait()

    @pl.when(has_low)
    def _():
        up.wait_recv()

    @pl.when(has_high)
    def _():
        down.wait_recv()

    for b in range(blocks):
        at = slice(b * TILE, (b + 1) * TILE)
        to = slice(centre + b * TILE, centre + (b + 1) * TILE)
        part = dot(swap, halo[:, at, :].reshape(side, ch)).astype(BF16)
        x[to, TILE:band, :] = part.reshape(TILE, TILE, ch)
    x[0:centre] = x[lon : lon + centre]
    x[lon + centre :] = x[centre : 2 * centre]

    weights = wf[...]

    @pl.loop(0, lon // 4)
    def _(q):
        for u in range(4):
            n = q * 4 + u
            window = x[pl.ds(n, taps)].reshape(taps * band, ch)
            f = dot(weights, window).astype(BF16)
            for k in range(kb):
                feat[pl.ds(pl.multiple_of(n * TILE, TILE), TILE), k * ch : (k + 1) * ch] = f[
                    k * TILE : (k + 1) * TILE
                ]

    for b in range(blocks):
        at = slice(b * TILE, (b + 1) * TILE)
        rows = slice(b * side, (b + 1) * side)
        pre = dot(feat[rows, :], mix[...])
        cot_t = dot(swap, cot[:, at, :].reshape(side, ch))
        cdf = 0.5 * (1.0 + lax.erf(pre * (0.5**0.5)))
        pdf = jnp.exp(-0.5 * pre * pre) * 0.3989422804014327
        h = (pre * cdf).astype(BF16)
        hidden[:, at, :] = dot(swap, h).astype(BF16).reshape(TILE, TILE, ch)
        pre_grad[rows, :] = (cot_t * (cdf + pre * pdf)).astype(BF16)

    def term(z, y, c):
        first = pl.multiple_of((4 * z + 2 * y + c) * shard, TILE)
        return mix_grad[pl.ds(first, shard), :]

    def by_core(z):
        return remote(c_out.at[z], c_in.at[z], c_send.at[z], c_recv.at[z], other_core)

    def by_row(z):
        return remote(y_out.at[z], y_in.at[z], y_send.at[z], y_recv.at[z], other_row)

    def by_depth(z):
        slot = (depth + 7 - z) % 4
        return remote(
            z_out.at[z], z_in.at[slot], z_send.at[z], z_recv.at[slot], 4 * z + me % 4
        )

    def send_core(z):
        for y in range(2):
            c_out[z, y] = term(z, y, 1 - core).astype(BF16)
        by_core(z).start()

    def send_row(z):
        by_core(z).wait_recv()
        y_out[z] = (term(z, 1 - row, core) + c_in[z, 1 - row].astype(F32)).astype(BF16)
        by_row(z).start()

    def send_depth(z):
        by_row(z).wait_recv()
        total = term(z, row, core) + c_in[z, row].astype(F32) + y_in[z].astype(F32)

        @pl.when(depth == z)
        def _():
            kept[...] = total

        @pl.when(depth != z)
        def _():
            z_out[z] = total.astype(BF16)
            by_depth(z).start()

    for k in range(kb):
        cols = slice(k * ch, (k + 1) * ch)
        mix_grad[cols, :] = dot(feat[:, cols], pre_grad[...], ((0,), (0,)))
        done = (k + 1) * ch // (4 * shard) - 1
        before = k * ch // (4 * shard) - 1
        if done > before:
            send_core(done)
            if done > 1:
                send_row(done - 2)

    for k in range(kb):
        fg = dot(pre_grad[...], mix[k * ch : (k + 1) * ch, :], ((1,), (1,))).astype(BF16)
        grads[:, k * TILE : (k + 1) * TILE, :] = fg.reshape(lon, TILE, ch)
        if k == 1:
            send_row(2)
        if k == 4:
            send_row(3)
        if k == 7:
            send_depth(0)
    acc[...] = jnp.zeros_like(acc)
    back = wb[...]

    def spread(q):
        for u in range(4):
            n = q * 4 + u
            at = pl.ds(pl.multiple_of(n * band, band), taps * band)
            acc[at, :] += dot(back, grads[n])

    pl.loop(0, lon // 16)(spread)
    send_depth(1)
    pl.loop(lon // 16, 3 * lon // 16)(spread)
    send_depth(2)
    pl.loop(3 * lon // 16, lon // 4)(spread)

    acc[lon * band : (lon + centre) * band, :] += acc[0 : centre * band, :]
    acc[centre * band : 2 * centre * band, :] += acc[(lon + centre) * band :, :]

    def block_of(b):
        blk = acc[(centre + b * TILE) * band : (centre + (b + 1) * TILE) * band, :]
        return blk.reshape(TILE, band, ch)

    for b in range(blocks):
        part = block_of(b)[:, TILE:, :].reshape(side, ch).astype(BF16)
        near[:, b * TILE : (b + 1) * TILE, :] = dot(swap, part).astype(BF16).reshape(TILE, TILE, ch)
    to_low = remote(
        near.at[0:reach], got.at[reach : 2 * reach], b_send.at[0], b_recv.at[0],
        me - 1,
    )
    to_high = remote(
        near.at[reach : 2 * reach], got.at[0:reach], b_send.at[1], b_recv.at[1],
        me + 1,
    )

    @pl.when(has_low)
    def _():
        to_low.start()

    @pl.when(has_high)
    def _():
        to_high.start()

    send_depth(3)
    for b in range(blocks):
        mine = block_of(b)[:, :TILE, :].reshape(side, ch)
        top = mine.astype(BF16)
        rest = (mine - top.astype(F32)).astype(BF16)
        own[:, b * TILE : (b + 1) * TILE, :] = (dot(swap, top) + dot(swap, rest)).reshape(
            TILE, TILE, ch
        )
    field_grad[reach : rows_dev - reach] = own[reach : rows_dev - reach].astype(BF16)

    @pl.when(has_high)
    def _():
        to_low.wait_recv()

    field_grad[rows_dev - reach :] = (
        own[rows_dev - reach :] + got[reach : 2 * reach].astype(F32)
    ).astype(BF16)

    @pl.when(has_low)
    def _():
        to_high.wait_recv()

    field_grad[0:reach] = (own[0:reach] + got[0:reach].astype(F32)).astype(BF16)

    total = kept[...]
    for slot in range(3):
        remote(
            z_out.at[0], z_in.at[slot], z_send.at[0], z_recv.at[slot], other_row
        ).wait_recv()
        total = total + z_in[slot].astype(F32)
    mix_shard[...] = total

    @pl.when(has_high)
    def _():
        up.wait_send()
        to_high.wait_send()

    @pl.when(has_low)
    def _():
        down.wait_send()
        to_low.wait_send()

    for z in range(4):
        by_core(z).wait_send()
        by_row(z).wait_send()

        @pl.when(depth != z)
        def _():
            by_depth(z).wait_send()


def fused(dims, field, basis, start, count, tap_count, mixing, cotangent):
    lon, ch, kb, taps, reach = dims
    rows_dev = field.shape[0]
    rows = rows_dev * lon
    shard = kb * ch // 16
    vmem = pl.BlockSpec(memory_space=pltpu.VMEM)
    hbm = pl.BlockSpec(memory_space=pl.ANY)
    smem = pl.BlockSpec(memory_space=pltpu.SMEM)
    band = 2 * TILE
    sems = pltpu.SemaphoreType.DMA
    return pl.pallas_call(
        lambda *refs: fused_kernel(dims, *refs),
        out_shape=(
            jax.ShapeDtypeStruct((rows_dev, lon, ch), BF16),
            jax.ShapeDtypeStruct((rows_dev, lon, ch), BF16),
            jax.ShapeDtypeStruct((shard, ch), F32),
        ),
        in_specs=[hbm, vmem, smem, smem, smem, hbm, hbm],
        out_specs=(vmem,) * 3,
        scratch_shapes=[
            pltpu.VMEM((kb * TILE, taps * band), BF16),
            pltpu.VMEM((taps * band, kb * TILE), BF16),
            pltpu.VMEM((rows_dev, lon, ch), BF16),
            pltpu.VMEM((kb * ch, ch), BF16),
            pltpu.VMEM((rows_dev, lon, ch), BF16),
            pltpu.VMEM((TILE, lon, ch), BF16),
            pltpu.VMEM((lon + taps - 1, band, ch), BF16),
            pltpu.VMEM((rows, kb * ch), BF16),
            pltpu.VMEM((rows, ch), BF16),
            pltpu.VMEM((kb * ch, ch), F32),
            pltpu.VMEM((lon, kb * TILE, ch), BF16),
            pltpu.VMEM(((lon + taps - 1) * band, ch), F32),
            pltpu.VMEM((rows_dev, lon, ch), F32),
            pltpu.VMEM((TILE, lon, ch), BF16),
            pltpu.VMEM((2 * reach, lon, ch), BF16),
            pltpu.VMEM((4, 2, shard, ch), BF16),
            pltpu.VMEM((4, 2, shard, ch), BF16),
            pltpu.VMEM((4, shard, ch), BF16),
            pltpu.VMEM((4, shard, ch), BF16),
            pltpu.VMEM((4, shard, ch), BF16),
            pltpu.VMEM((3, shard, ch), BF16),
            pltpu.VMEM((shard, ch), F32),
            sems((3,)), sems((2,)), sems((2,)), sems((2,)), sems((2,)), sems((4,)),
            sems((4,)), sems((4,)), sems((4,)), sems((4,)), sems((3,)),
        ],
        compiler_params=pltpu.CompilerParams(
            vmem_limit_bytes=48 * 2**20, collective_id=0, has_side_effects=True
        ),
        cost_estimate=pl.CostEstimate(
            flops=10 * rows * kb * ch * ch, bytes_accessed=8 * 2**20, transcendentals=2 * rows * ch
        ),
        name="conv_and_gradients",
    )(
        field,
        basis.transpose(1, 3, 0, 2).reshape(basis.shape[1], kb * rows_dev, taps),
        start,
        count,
        tap_count,
        mixing,
        cotangent,
    )


def local(field, row_start, row_count, tap_count, basis, mixing, cotangent):
    rows_dev, lon, ch = field.shape
    slots, taps, kb = basis.shape[1:]
    reach = (slots - 1) // 2
    band = 2 * TILE
    dims = (lon, ch, kb, taps, reach)
    centre = taps // 2
    if lax.axis_size("lat") == 16:
        return fused(dims, field, basis, row_start, row_count, tap_count, mixing, cotangent)

    first_row = lax.axis_index("lat") * rows_dev - reach
    slot_ids = jnp.arange(slots, dtype=jnp.int32)
    tap_ids = jnp.arange(taps, dtype=jnp.int32)
    at_row = (row_start - first_row)[:, None] + slot_ids[None, :]
    place = jnp.where(
        at_row < reach,
        at_row + TILE,
        jnp.where(at_row < reach + rows_dev, at_row - reach, at_row),
    )
    placing = (place[:, :, None] == jnp.arange(band, dtype=jnp.int32)) & (
        slot_ids[None, :] < row_count[:, None]
    )[:, :, None]
    tap_mask = jnp.abs(tap_ids - centre)[None, :] <= (tap_count // 2)[:, None]
    masked = jnp.where(tap_mask[:, None, :, None], basis, jnp.zeros((), BF16))
    placed = lax.dot_general(
        masked.reshape(rows_dev, slots, taps * kb),
        placing.astype(BF16),
        (((1,), (1,)), ((0,), (0,))),
        preferred_element_type=F32,
    ).astype(BF16)
    placed = placed.reshape(rows_dev, taps, kb, band)
    wf = placed.transpose(2, 0, 1, 3).reshape(kb * rows_dev, taps * band)
    wb = wf.T

    low_in = from_behind(field[rows_dev - reach :], "lat", 1)
    high_in = from_behind(field[:reach], "lat", -1)
    rows = rows_dev * lon
    vmem = pl.BlockSpec(memory_space=pltpu.VMEM)
    hidden, pre_grad, mix_part = pl.pallas_call(
        lambda *refs: fwd_kernel(dims, *refs),
        out_shape=(
            jax.ShapeDtypeStruct((rows_dev, lon, ch), BF16),
            jax.ShapeDtypeStruct((rows, ch), BF16),
            jax.ShapeDtypeStruct((kb * ch, ch), F32),
        ),
        in_specs=[vmem] * 6,
        out_specs=(vmem,) * 3,
        scratch_shapes=[
            pltpu.VMEM(((lon + taps - 1) * band, ch), BF16),
            pltpu.VMEM((rows, kb * ch), BF16),
            pltpu.VMEM((TILE, lon, ch), BF16),
        ],
        compiler_params=pltpu.CompilerParams(vmem_limit_bytes=40 * 2**20),
        cost_estimate=pl.CostEstimate(
            flops=6 * rows * kb * ch * ch, bytes_accessed=8 * 2**20, transcendentals=2 * rows * ch
        ),
        name="features_hidden_mixing_grad",
    )(field, low_in, high_in, wf, mixing, cotangent)

    own, low, high = pl.pallas_call(
        lambda *refs: bwd_kernel(dims, *refs),
        out_shape=(
            jax.ShapeDtypeStruct((rows_dev, lon, ch), F32),
            jax.ShapeDtypeStruct((reach, lon, ch), BF16),
            jax.ShapeDtypeStruct((reach, lon, ch), BF16),
        ),
        in_specs=[vmem] * 3,
        out_specs=(vmem,) * 3,
        scratch_shapes=[
            pltpu.VMEM((lon, kb * TILE, ch), BF16),
            pltpu.VMEM(((lon + taps - 1) * band, ch), F32),
        ],
        compiler_params=pltpu.CompilerParams(vmem_limit_bytes=40 * 2**20),
        cost_estimate=pl.CostEstimate(
            flops=4 * rows * kb * ch * ch, bytes_accessed=8 * 2**20, transcendentals=0
        ),
        name="field_grad_of_band",
    )(pre_grad, mixing, wb)

    mixing_grad = lax.psum_scatter(mix_part, "lat", scatter_dimension=0, tiled=True)
    from_high = from_behind(low, "lat", -1).astype(F32)
    from_low = from_behind(high, "lat", 1).astype(F32)
    filler = jnp.zeros((rows_dev - reach, lon, ch), F32)
    field_grad = (
        own
        + jnp.concatenate([filler, from_high], axis=0)
        + jnp.concatenate([from_low, filler], axis=0)
    ).astype(BF16)
    return (hidden, field_grad, mixing_grad)


def solution(mesh):
    placed = (
        P(("member", "lat"), None, None),
        P("lat"),
        P("lat"),
        P("lat"),
        P("lat", None, None, None),
        P(),
        P(("member", "lat"), None, None),
    )
    return jax.shard_map(
        local,
        mesh=mesh,
        in_specs=placed,
        out_specs=(
            P(("member", "lat"), None, None),
            P(("member", "lat"), None, None),
            P(("member", "lat"), None),
        ),
        check_vma=False,
    )
```

```python
import jax
import jax.numpy as jnp
from jax import lax
from jax.experimental import pallas as pl
from jax.experimental.pallas import tpu as pltpu
from jax.sharding import PartitionSpec as P

BF16 = jnp.bfloat16
F32 = jnp.float32
TILE = 16


def from_behind(block, axis, distance):
    devices = range(lax.axis_size(axis))
    route = [(i - distance, i) for i in devices if i - distance in devices]
    return lax.ppermute(block, axis, route)


def dot(a, b, dims=((1,), (0,))):
    return lax.dot_general(a, b, (dims, ((), ())), preferred_element_type=F32)


def swap_matrix():
    side = TILE * TILE
    row = lax.broadcasted_iota(jnp.int32, (side, side), 0)
    col = lax.broadcasted_iota(jnp.int32, (side, side), 1)
    return jnp.where((row & (TILE - 1)) * TILE + (row >> 4) == col, 1.0, 0.0).astype(BF16)


def fwd_kernel(dims, field, low, high, wf, mix, cot, hidden, pre_grad, mix_grad, x, feat, halo):
    lon, ch, kb, taps, reach = dims
    centre = taps // 2
    band = 2 * TILE
    blocks = lon // TILE
    side = TILE * TILE
    swap = swap_matrix()
    halo[0:reach] = low[...]
    halo[reach : 2 * reach] = high[...]
    halo[2 * reach :] = jnp.zeros((TILE - 2 * reach, lon, ch), BF16)
    for b in range(blocks):
        at = slice(b * TILE, (b + 1) * TILE)
        own_t = dot(swap, field[:, at, :].reshape(side, ch)).astype(BF16)
        halo_t = dot(swap, halo[:, at, :].reshape(side, ch)).astype(BF16)
        both = jnp.concatenate(
            [own_t.reshape(TILE, TILE, ch), halo_t.reshape(TILE, TILE, ch)], axis=1
        )
        x[(centre + b * TILE) * band : (centre + (b + 1) * TILE) * band, :] = both.reshape(
            TILE * band, ch
        )
    x[0 : centre * band, :] = x[lon * band : (lon + centre) * band, :]
    x[(lon + centre) * band :, :] = x[centre * band : 2 * centre * band, :]

    weights = wf[...]

    @pl.loop(0, lon // 4)
    def _(q):
        for u in range(4):
            n = q * 4 + u
            window = x[pl.ds(pl.multiple_of(n * band, band), taps * band), :]
            f = dot(weights, window).astype(BF16)
            for k in range(kb):
                feat[pl.ds(pl.multiple_of(n * TILE, TILE), TILE), k * ch : (k + 1) * ch] = f[
                    k * TILE : (k + 1) * TILE
                ]

    for b in range(blocks):
        at = slice(b * TILE, (b + 1) * TILE)
        rows = slice(b * side, (b + 1) * side)
        pre = dot(feat[rows, :], mix[...])
        cot_t = dot(swap, cot[:, at, :].reshape(side, ch))
        cdf = 0.5 * (1.0 + lax.erf(pre * (0.5**0.5)))
        pdf = jnp.exp(-0.5 * pre * pre) * 0.3989422804014327
        h = (pre * cdf).astype(BF16)
        hidden[:, at, :] = dot(swap, h).astype(BF16).reshape(TILE, TILE, ch)
        pre_grad[rows, :] = (cot_t * (cdf + pre * pdf)).astype(BF16)
    for k in range(kb):
        cols = slice(k * ch, (k + 1) * ch)
        mix_grad[cols, :] = dot(feat[:, cols], pre_grad[...], ((0,), (0,)))


def bwd_kernel(dims, pre_grad, mix, wb, own, low, high, grads, acc):
    lon, ch, kb, taps, reach = dims
    centre = taps // 2
    band = 2 * TILE
    blocks = lon // TILE
    side = TILE * TILE
    swap = swap_matrix()
    for k in range(kb):
        fg = dot(pre_grad[...], mix[k * ch : (k + 1) * ch, :], ((1,), (1,))).astype(BF16)
        grads[:, k * TILE : (k + 1) * TILE, :] = fg.reshape(lon, TILE, ch)
    acc[...] = jnp.zeros_like(acc)
    weights = wb[...]

    @pl.loop(0, lon // 4)
    def _(q):
        for u in range(4):
            n = q * 4 + u
            at = pl.ds(pl.multiple_of(n * band, band), taps * band)
            acc[at, :] += dot(weights, grads[n])

    acc[lon * band : (lon + centre) * band, :] += acc[0 : centre * band, :]
    acc[centre * band : 2 * centre * band, :] += acc[(lon + centre) * band :, :]
    for b in range(blocks):
        at = slice(b * TILE, (b + 1) * TILE)
        blk = acc[(centre + b * TILE) * band : (centre + (b + 1) * TILE) * band, :]
        blk = blk.reshape(TILE, band, ch)
        mine = blk[:, :TILE, :].reshape(side, ch)
        top = mine.astype(BF16)
        rest = (mine - top.astype(F32)).astype(BF16)
        own[:, at, :] = (dot(swap, top) + dot(swap, rest)).reshape(TILE, TILE, ch)
        near = dot(swap, blk[:, TILE:, :].reshape(side, ch).astype(BF16)).astype(BF16)
        near = near.reshape(TILE, TILE, ch)
        low[:, at, :] = near[:reach]
        high[:, at, :] = near[reach : 2 * reach]


def filter_matrix(dims, basis, start, count, tap_count, first_row):
    lon, ch, kb, taps, reach = dims
    slots = basis.shape[0]
    band = 2 * TILE
    lanes = taps * band
    out_row = lax.broadcasted_iota(jnp.int32, (TILE, lanes), 0)
    lane = lax.broadcasted_iota(jnp.int32, (TILE, lanes), 1)
    place = lane & (band - 1)
    tap = lane >> 5
    in_row = jnp.where(
        place < TILE, place + reach, jnp.where(place < TILE + reach, place - TILE, place)
    )
    first = jnp.zeros((TILE, lanes), jnp.int32)
    used = first
    half = first
    for o in range(TILE):
        here = out_row == o
        first = jnp.where(here, start[o] - first_row, first)
        used = jnp.where(here, count[o], used)
        half = jnp.where(here, tap_count[o] >> 1, half)
    slot = in_row - first
    inside = (slot < used) & (jnp.abs(tap - taps // 2) <= half) & (place < TILE + 2 * reach)
    slot = jnp.where(inside, slot, -1)
    slot = jnp.concatenate([slot] * kb, axis=0)
    to_lane = lax.broadcasted_iota(jnp.int32, (taps, lanes), 1) >> 5
    spread = jnp.where(
        lax.broadcasted_iota(jnp.int32, (taps, lanes), 0) == to_lane, 1.0, 0.0
    ).astype(BF16)
    total = jnp.zeros((kb * TILE, lanes), F32)
    for j in range(slots):
        total = jnp.where(slot == j, dot(basis[j], spread), total)
    return total.astype(BF16)


def remote(src, dst, send, recv, target):
    return pltpu.make_async_remote_copy(
        src_ref=src,
        dst_ref=dst,
        send_sem=send,
        recv_sem=recv,
        device_id={"lat": target},
        device_id_type=pl.DeviceIdType.MESH,
    )


def fused_kernel(
    dims, field_in, basis, start_in, count_in, taps_in, mix_in, cot_in, hidden, field_grad, mix_shard,
    start, count, tap_count, wf, wb, field, mix, cot, halo, x, feat, pre_grad, mix_grad, grads, acc, own,
    near, got, c_out, c_in, y_out, y_in, z_out, z_in, kept,
    l_sem, f_send, f_recv, b_send, b_recv, c_send, c_recv, y_send, y_recv, z_send, z_recv,
):
    lon, ch, kb, taps, reach = dims
    centre = taps // 2
    band = 2 * TILE
    blocks = lon // TILE
    side = TILE * TILE
    rows_dev = field.shape[0]
    shard = mix_shard.shape[0]
    me = lax.axis_index("lat")
    last = lax.axis_size("lat") - 1
    core = me % 2
    row = (me // 2) % 2
    depth = me // 4
    other_core = me + 1 - 2 * core
    other_row = me + 2 - 4 * row
    far = me - 1 + 2 * core
    has_far = (far >= 0) & (far <= last)
    has_low = me > 0
    has_high = me < last

    loads = [
        pltpu.make_async_copy(src, dst, l_sem.at[i])
        for i, (src, dst) in enumerate(
            (
                (field_in, field),
                (cot_in, cot),
                (mix_in, mix),
                (start_in, start),
                (count_in, count),
                (taps_in, tap_count),
            )
        )
    ]
    for load in loads:
        load.start()

    barrier = pltpu.get_barrier_semaphore()

    def greet(device):
        pl.semaphore_signal(
            barrier, inc=1, device_id={"lat": device}, device_id_type=pl.DeviceIdType.MESH
        )

    greet(other_core)
    greet(other_row)
    for step in (1, 2, 3):
        greet((me + 4 * step) % 16)

    @pl.when(has_far)
    def _():
        greet(far)

    pl.semaphore_wait(barrier, 5 + has_far.astype(jnp.int32))

    up = remote(
        field_in.at[rows_dev - reach : rows_dev], halo.at[0:reach], f_send.at[0], f_recv.at[0],
        me + 1,
    )
    down = remote(
        field_in.at[0:reach], halo.at[reach : 2 * reach], f_send.at[1], f_recv.at[1],
        me - 1,
    )

    @pl.when(has_high)
    def _():
        up.start()

    @pl.when(has_low)
    def _():
        down.start()

    none = jnp.zeros((reach, lon, ch), BF16)

    @pl.when(me == 0)
    def _():
        halo[0:reach] = none
        got[0:reach] = none

    @pl.when(me == last)
    def _():
        halo[reach : 2 * reach] = none
        got[reach : 2 * reach] = none

    halo[2 * reach :] = jnp.zeros((TILE - 2 * reach, lon, ch), BF16)
    swap = swap_matrix()
    loads[0].wait()
    for b in range(blocks):
        at = slice(b * TILE, (b + 1) * TILE)
        to = slice(centre + b * TILE, centre + (b + 1) * TILE)
        part = dot(swap, field[:, at, :].reshape(side, ch)).astype(BF16)
        x[to, 0:TILE, :] = part.reshape(TILE, TILE, ch)
    for load in loads[3:]:
        load.wait()
    wf[...] = filter_matrix(dims, basis, start, count, tap_count, me * rows_dev - reach)
    side_k = kb * TILE
    eye = jnp.where(
        lax.broadcasted_iota(jnp.int32, (side_k, side_k), 0)
        == lax.broadcasted_iota(jnp.int32, (side_k, side_k), 1),
        1.0,
        0.0,
    ).astype(BF16)
    wb[...] = dot(wf[...], eye, ((0,), (0,))).astype(BF16)
    loads[1].wait()
    loads[2].wait()

    @pl.when(has_low)
    def _():
        up.wait_recv()

    @pl.when(has_high)
    def _():
        down.wait_recv()

    for b in range(blocks):
        at = slice(b * TILE, (b + 1) * TILE)
        to = slice(centre + b * TILE, centre + (b + 1) * TILE)
        part = dot(swap, halo[:, at, :].reshape(side, ch)).astype(BF16)
        x[to, TILE:band, :] = part.reshape(TILE, TILE, ch)
    x[0:centre] = x[lon : lon + centre]
    x[lon + centre :] = x[centre : 2 * centre]

    weights = wf[...]

    @pl.loop(0, lon // 4)
    def _(q):
        for u in range(4):
            n = q * 4 + u
            window = x[pl.ds(n, taps)].reshape(taps * band, ch)
            f = dot(weights, window).astype(BF16)
            for k in range(kb):
                feat[pl.ds(pl.multiple_of(n * TILE, TILE), TILE), k * ch : (k + 1) * ch] = f[
                    k * TILE : (k + 1) * TILE
                ]

    for b in range(blocks):
        at = slice(b * TILE, (b + 1) * TILE)
        rows = slice(b * side, (b + 1) * side)
        pre = dot(feat[rows, :], mix[...])
        cot_t = dot(swap, cot[:, at, :].reshape(side, ch))
        cdf = 0.5 * (1.0 + lax.erf(pre * (0.5**0.5)))
        pdf = jnp.exp(-0.5 * pre * pre) * 0.3989422804014327
        h = (pre * cdf).astype(BF16)
        hidden[:, at, :] = dot(swap, h).astype(BF16).reshape(TILE, TILE, ch)
        pre_grad[rows, :] = (cot_t * (cdf + pre * pdf)).astype(BF16)

    def term(z, y, c):
        first = pl.multiple_of((4 * z + 2 * y + c) * shard, TILE)
        return mix_grad[pl.ds(first, shard), :]

    def by_core(z):
        return remote(c_out.at[z], c_in.at[z], c_send.at[z], c_recv.at[z], other_core)

    def by_row(z):
        return remote(y_out.at[z], y_in.at[z], y_send.at[z], y_recv.at[z], other_row)

    def by_depth(z):
        slot = (depth + 7 - z) % 4
        return remote(
            z_out.at[z], z_in.at[slot], z_send.at[z], z_recv.at[slot], 4 * z + me % 4
        )

    def send_core(z):
        for y in range(2):
            c_out[z, y] = term(z, y, 1 - core).astype(BF16)
        by_core(z).start()

    def send_row(z):
        by_core(z).wait_recv()
        y_out[z] = (term(z, 1 - row, core) + c_in[z, 1 - row].astype(F32)).astype(BF16)
        by_row(z).start()

    def send_depth(z):
        by_row(z).wait_recv()
        total = term(z, row, core) + c_in[z, row].astype(F32) + y_in[z].astype(F32)

        @pl.when(depth == z)
        def _():
            kept[...] = total

        @pl.when(depth != z)
        def _():
            z_out[z] = total.astype(BF16)
            by_depth(z).start()

    for k in range(kb):
        cols = slice(k * ch, (k + 1) * ch)
        mix_grad[cols, :] = dot(feat[:, cols], pre_grad[...], ((0,), (0,)))
        done = (k + 1) * ch // (4 * shard) - 1
        before = k * ch // (4 * shard) - 1
        if done > before:
            send_core(done)
            if done > 1:
                send_row(done - 2)

    for k in range(kb):
        fg = dot(pre_grad[...], mix[k * ch : (k + 1) * ch, :], ((1,), (1,))).astype(BF16)
        grads[:, k * TILE : (k + 1) * TILE, :] = fg.reshape(lon, TILE, ch)
        if k == 1:
            send_row(2)
        if k == 4:
            send_row(3)
        if k == 7:
            send_depth(0)
    acc[...] = jnp.zeros_like(acc)
    back = wb[...]

    def spread(q):
        for u in range(4):
            n = q * 4 + u
            at = pl.ds(pl.multiple_of(n * band, band), taps * band)
            acc[at, :] += dot(back, grads[n])

    pl.loop(0, lon // 16)(spread)
    send_depth(1)
    pl.loop(lon // 16, 3 * lon // 16)(spread)
    send_depth(2)
    pl.loop(3 * lon // 16, lon // 4)(spread)

    acc[lon * band : (lon + centre) * band, :] += acc[0 : centre * band, :]
    acc[centre * band : 2 * centre * band, :] += acc[(lon + centre) * band :, :]

    def block_of(b):
        blk = acc[(centre + b * TILE) * band : (centre + (b + 1) * TILE) * band, :]
        return blk.reshape(TILE, band, ch)

    for b in range(blocks):
        part = block_of(b)[:, TILE:, :].reshape(side, ch).astype(BF16)
        near[:, b * TILE : (b + 1) * TILE, :] = dot(swap, part).astype(BF16).reshape(TILE, TILE, ch)
    to_low = remote(
        near.at[0:reach], got.at[reach : 2 * reach], b_send.at[0], b_recv.at[0],
        me - 1,
    )
    to_high = remote(
        near.at[reach : 2 * reach], got.at[0:reach], b_send.at[1], b_recv.at[1],
        me + 1,
    )

    @pl.when(has_low)
    def _():
        to_low.start()

    @pl.when(has_high)
    def _():
        to_high.start()

    send_depth(3)
    for b in range(blocks):
        mine = block_of(b)[:, :TILE, :].reshape(side, ch)
        top = mine.astype(BF16)
        rest = (mine - top.astype(F32)).astype(BF16)
        own[:, b * TILE : (b + 1) * TILE, :] = (dot(swap, top) + dot(swap, rest)).reshape(
            TILE, TILE, ch
        )
    field_grad[reach : rows_dev - reach] = own[reach : rows_dev - reach].astype(BF16)

    @pl.when(has_high)
    def _():
        to_low.wait_recv()

    field_grad[rows_dev - reach :] = (
        own[rows_dev - reach :] + got[reach : 2 * reach].astype(F32)
    ).astype(BF16)

    @pl.when(has_low)
    def _():
        to_high.wait_recv()

    field_grad[0:reach] = (own[0:reach] + got[0:reach].astype(F32)).astype(BF16)

    total = kept[...]
    for slot in range(3):
        remote(
            z_out.at[0], z_in.at[slot], z_send.at[0], z_recv.at[slot], other_row
        ).wait_recv()
        total = total + z_in[slot].astype(F32)
    mix_shard[...] = total

    @pl.when(has_high)
    def _():
        up.wait_send()
        to_high.wait_send()

    @pl.when(has_low)
    def _():
        down.wait_send()
        to_low.wait_send()

    for z in range(4):
        by_core(z).wait_send()
        by_row(z).wait_send()

        @pl.when(depth != z)
        def _():
            by_depth(z).wait_send()


def fused(dims, field, basis, start, count, tap_count, mixing, cotangent):
    lon, ch, kb, taps, reach = dims
    rows_dev = field.shape[0]
    rows = rows_dev * lon
    shard = kb * ch // 16
    vmem = pl.BlockSpec(memory_space=pltpu.VMEM)
    hbm = pl.BlockSpec(memory_space=pl.ANY)
    band = 2 * TILE
    sems = pltpu.SemaphoreType.DMA
    return pl.pallas_call(
        lambda *refs: fused_kernel(dims, *refs),
        out_shape=(
            jax.ShapeDtypeStruct((rows_dev, lon, ch), BF16),
            jax.ShapeDtypeStruct((rows_dev, lon, ch), BF16),
            jax.ShapeDtypeStruct((shard, ch), F32),
        ),
        in_specs=[hbm, vmem, hbm, hbm, hbm, hbm, hbm],
        out_specs=(vmem,) * 3,
        scratch_shapes=[
            pltpu.SMEM((rows_dev,), jnp.int32),
            pltpu.SMEM((rows_dev,), jnp.int32),
            pltpu.SMEM((rows_dev,), jnp.int32),
            pltpu.VMEM((kb * TILE, taps * band), BF16),
            pltpu.VMEM((taps * band, kb * TILE), BF16),
            pltpu.VMEM((rows_dev, lon, ch), BF16),
            pltpu.VMEM((kb * ch, ch), BF16),
            pltpu.VMEM((rows_dev, lon, ch), BF16),
            pltpu.VMEM((TILE, lon, ch), BF16),
            pltpu.VMEM((lon + taps - 1, band, ch), BF16),
            pltpu.VMEM((rows, kb * ch), BF16),
            pltpu.VMEM((rows, ch), BF16),
            pltpu.VMEM((kb * ch, ch), F32),
            pltpu.VMEM((lon, kb * TILE, ch), BF16),
            pltpu.VMEM(((lon + taps - 1) * band, ch), F32),
            pltpu.VMEM((rows_dev, lon, ch), F32),
            pltpu.VMEM((TILE, lon, ch), BF16),
            pltpu.VMEM((2 * reach, lon, ch), BF16),
            pltpu.VMEM((4, 2, shard, ch), BF16),
            pltpu.VMEM((4, 2, shard, ch), BF16),
            pltpu.VMEM((4, shard, ch), BF16),
            pltpu.VMEM((4, shard, ch), BF16),
            pltpu.VMEM((4, shard, ch), BF16),
            pltpu.VMEM((3, shard, ch), BF16),
            pltpu.VMEM((shard, ch), F32),
            sems((6,)), sems((2,)), sems((2,)), sems((2,)), sems((2,)), sems((4,)),
            sems((4,)), sems((4,)), sems((4,)), sems((4,)), sems((3,)),
        ],
        compiler_params=pltpu.CompilerParams(
            vmem_limit_bytes=62 * 2**20, collective_id=0, has_side_effects=True
        ),
        cost_estimate=pl.CostEstimate(
            flops=10 * rows * kb * ch * ch, bytes_accessed=8 * 2**20, transcendentals=2 * rows * ch
        ),
        name="conv_and_gradients",
    )(
        field,
        basis.transpose(1, 3, 0, 2).reshape(basis.shape[1], kb * rows_dev, taps),
        start,
        count,
        tap_count,
        mixing,
        cotangent,
    )


def local(field, row_start, row_count, tap_count, basis, mixing, cotangent):
    rows_dev, lon, ch = field.shape
    slots, taps, kb = basis.shape[1:]
    reach = (slots - 1) // 2
    band = 2 * TILE
    dims = (lon, ch, kb, taps, reach)
    centre = taps // 2
    if lax.axis_size("lat") == 16:
        return fused(dims, field, basis, row_start, row_count, tap_count, mixing, cotangent)

    first_row = lax.axis_index("lat") * rows_dev - reach
    slot_ids = jnp.arange(slots, dtype=jnp.int32)
    tap_ids = jnp.arange(taps, dtype=jnp.int32)
    at_row = (row_start - first_row)[:, None] + slot_ids[None, :]
    place = jnp.where(
        at_row < reach,
        at_row + TILE,
        jnp.where(at_row < reach + rows_dev, at_row - reach, at_row),
    )
    placing = (place[:, :, None] == jnp.arange(band, dtype=jnp.int32)) & (
        slot_ids[None, :] < row_count[:, None]
    )[:, :, None]
    tap_mask = jnp.abs(tap_ids - centre)[None, :] <= (tap_count // 2)[:, None]
    masked = jnp.where(tap_mask[:, None, :, None], basis, jnp.zeros((), BF16))
    placed = lax.dot_general(
        masked.reshape(rows_dev, slots, taps * kb),
        placing.astype(BF16),
        (((1,), (1,)), ((0,), (0,))),
        preferred_element_type=F32,
    ).astype(BF16)
    placed = placed.reshape(rows_dev, taps, kb, band)
    wf = placed.transpose(2, 0, 1, 3).reshape(kb * rows_dev, taps * band)
    wb = wf.T

    low_in = from_behind(field[rows_dev - reach :], "lat", 1)
    high_in = from_behind(field[:reach], "lat", -1)
    rows = rows_dev * lon
    vmem = pl.BlockSpec(memory_space=pltpu.VMEM)
    hidden, pre_grad, mix_part = pl.pallas_call(
        lambda *refs: fwd_kernel(dims, *refs),
        out_shape=(
            jax.ShapeDtypeStruct((rows_dev, lon, ch), BF16),
            jax.ShapeDtypeStruct((rows, ch), BF16),
            jax.ShapeDtypeStruct((kb * ch, ch), F32),
        ),
        in_specs=[vmem] * 6,
        out_specs=(vmem,) * 3,
        scratch_shapes=[
            pltpu.VMEM(((lon + taps - 1) * band, ch), BF16),
            pltpu.VMEM((rows, kb * ch), BF16),
            pltpu.VMEM((TILE, lon, ch), BF16),
        ],
        compiler_params=pltpu.CompilerParams(vmem_limit_bytes=40 * 2**20),
        cost_estimate=pl.CostEstimate(
            flops=6 * rows * kb * ch * ch, bytes_accessed=8 * 2**20, transcendentals=2 * rows * ch
        ),
        name="features_hidden_mixing_grad",
    )(field, low_in, high_in, wf, mixing, cotangent)

    own, low, high = pl.pallas_call(
        lambda *refs: bwd_kernel(dims, *refs),
        out_shape=(
            jax.ShapeDtypeStruct((rows_dev, lon, ch), F32),
            jax.ShapeDtypeStruct((reach, lon, ch), BF16),
            jax.ShapeDtypeStruct((reach, lon, ch), BF16),
        ),
        in_specs=[vmem] * 3,
        out_specs=(vmem,) * 3,
        scratch_shapes=[
            pltpu.VMEM((lon, kb * TILE, ch), BF16),
            pltpu.VMEM(((lon + taps - 1) * band, ch), F32),
        ],
        compiler_params=pltpu.CompilerParams(vmem_limit_bytes=40 * 2**20),
        cost_estimate=pl.CostEstimate(
            flops=4 * rows * kb * ch * ch, bytes_accessed=8 * 2**20, transcendentals=0
        ),
        name="field_grad_of_band",
    )(pre_grad, mixing, wb)

    mixing_grad = lax.psum_scatter(mix_part, "lat", scatter_dimension=0, tiled=True)
    from_high = from_behind(low, "lat", -1).astype(F32)
    from_low = from_behind(high, "lat", 1).astype(F32)
    filler = jnp.zeros((rows_dev - reach, lon, ch), F32)
    field_grad = (
        own
        + jnp.concatenate([filler, from_high], axis=0)
        + jnp.concatenate([from_low, filler], axis=0)
    ).astype(BF16)
    return (hidden, field_grad, mixing_grad)


def solution(mesh):
    placed = (
        P(("member", "lat"), None, None),
        P("lat"),
        P("lat"),
        P("lat"),
        P("lat", None, None, None),
        P(),
        P(("member", "lat"), None, None),
    )
    return jax.shard_map(
        local,
        mesh=mesh,
        in_specs=placed,
        out_specs=(
            P(("member", "lat"), None, None),
            P(("member", "lat"), None, None),
            P(("member", "lat"), None),
        ),
        check_vma=False,
    )
```
